32 devices in a mesh: groups: 2 (over x), img: 8 (over z, y), head: 2 (over core).
Axes of the slice: x: 2, y: 2, z: 4, core: 2. Of those that a mesh axis runs over, the one named last changes fastest.
Arguments:
- enc_tokens: bfloat16 [64, 32, 1024], P(('groups', 'img')), parts along dimension 0
- pairs: int32 [256, 2], P('groups'), parts along dimension 0, may hold values from 0 to 31, as said below
- live: int32 [16], P('groups'), parts along dimension 0, may hold values from 1 to 16, as said below
- proj_w: bfloat16 [1024, 768], replicated, may hold values from -0.1875 to 0.1875
- self_qkv: bfloat16 [768, 3, 768], P(None, None, 'head')
- self_out: bfloat16 [768, 768], P('head'), may hold values from -0.21875 to 0.21875
- cross_q: bfloat16 [768, 768], P(None, 'head')
- cross_kv: bfloat16 [768, 2, 768], P(None, None, 'head')
- cross_out: bfloat16 [768, 768], P('head'), may hold values from -0.21875 to 0.21875
- mlp_w1: bfloat16 [768, 3072], P(None, 'head'), may hold values from -0.21875 to 0.21875
- mlp_w2: bfloat16 [3072, 768], P('head'), may hold values from -0.109375 to 0.109375
- head_w: bfloat16 [768, 3712], P('img', 'head'), may hold values from -0.21875 to 0.21875
Outputs:
- joined_out: float32 [64, 3712, 32], P(('groups', 'img'), 'head'), parts along dimension 0
The draws below stay inside these ranges and needn't reach their ends.
There are 2 independent parts, one for each index of `groups`. The reference program is written for one: setup_inputs(seed, part) draws one part's arguments, and reference() takes and returns one part's arrays. A program takes and returns all parts, laid end to end along the dimension named above; an argument that names none is the same for every part. Nothing has to cross between parts.
Inputs may be any that keep to these rules, and one draw needn't show every extreme that they name: `pairs`: rows o * 16 to o * 16 + 15 are the pair slots of owner o. The two images of a pair differ. Image i is held by img index i // 4. Among the 2 * live[o] pair sides of owner o's live slots, at most 4 name images held by one img index, and some owner reaches 4. `live`: some owner uses all 16 slots.
All inputs are finite; a program needn't handle non-finite values.
Results may differ from the reference program's by a relative error of at most 0.012.
Values may be sent and summed in bfloat16 or wider, within the bound.
A program may use at most 128 MiB of HBM per device.

```python
import jax
import jax.numpy as jnp
from jax import lax

D = 768
E = 1024
FF = 3072
HD = 64
OUTC = 3712
TOK = 32
IMG_DEV = 4
CAP = 16
IMAGES = 32
N_IMG = 8


def query_matrix(key):
    return jax.random.normal(jax.random.fold_in(key, 31), (D, D), jnp.float32) * D ** (-0.5)


def draw_enc_tokens(key, part):
    key = jax.random.fold_in(key, 11)
    own_key, spread_key = jax.random.split(key)
    own_part = jnp.clip(jax.random.normal(own_key, (IMAGES, TOK, E), jnp.float32), -6.0, 6.0)
    scales = jnp.exp(jax.random.uniform(spread_key, (IMAGES, 1, 1), jnp.float32, 0.0, 2.3))
    return (own_part * scales).astype(jnp.bfloat16)


def draw_self_qkv(key, part):
    key = jax.random.fold_in(key, 21)
    matrix_key = jax.random.fold_in(key, 0)
    matrix = jax.random.normal(matrix_key, (D, 3, D), jnp.float32) * D ** (-0.5)
    return matrix.astype(jnp.bfloat16)


def draw_cross_q(key, part):
    shared = query_matrix(key)
    return shared.astype(jnp.bfloat16)


def draw_cross_kv(key, part):
    key = jax.random.fold_in(key, 33)
    matrix_key = jax.random.fold_in(key, 0)
    matrix = jax.random.normal(matrix_key, (D, 2, D), jnp.float32) * D ** (-0.5)
    matrix = matrix.at[:, 1, :].multiply(4.0)
    return matrix.astype(jnp.bfloat16)


def permuted(subkey):
    return jax.random.permutation(subkey, N_IMG)


def draw_pairs(key, part):
    key = jax.random.fold_in(key, 7)
    subkeys = jax.random.split(key, N_IMG + 1)
    orders = jax.vmap(permuted)(subkeys[:N_IMG])
    spot_ids = jnp.broadcast_to((jnp.arange(2 * CAP) % N_IMG)[None, :], (N_IMG, 2 * CAP))
    source = jnp.take_along_axis(orders, spot_ids, axis=1)
    within = jax.random.randint(subkeys[N_IMG], (N_IMG, 2 * CAP), 0, IMG_DEV)
    return (source * IMG_DEV + within).astype(jnp.int32).reshape(N_IMG * CAP, 2)


def draw_live(key, part):
    key = jax.random.fold_in(key, 5)
    count_key, busy_key = jax.random.split(key)
    counts = jax.random.randint(count_key, (N_IMG,), 1, CAP + 1)
    busiest = jax.random.randint(busy_key, (), 0, N_IMG)
    return jnp.where(jnp.arange(N_IMG) == busiest, CAP, counts).astype(jnp.int32)


def level_of(stream_key, dims, cuts, smallest, top_value):
    def one(axis_at, parts):
        draws = jax.random.uniform(jax.random.fold_in(jax.random.fold_in(stream_key, 6), axis_at), (parts,), jnp.float32, smallest / len(cuts), top_value / len(cuts))
        return jnp.repeat(jnp.exp(draws), dims[axis_at] // parts).reshape((-1,) + (1,) * (len(dims) - axis_at - 1))

    gain = one(*cuts[0])
    for cut in cuts[1:]:
        gain = gain * one(*cut)
    return gain


def noise(stream_key, dims, spread, bound, cuts=(), held_as=jnp.bfloat16):
    gain = level_of(stream_key, dims, cuts, -0.22, 0.18) if cuts else 1.0
    array = jax.random.normal(stream_key, dims, jnp.float32) * spread * gain
    return jnp.minimum(jnp.maximum(array, -bound), bound).astype(held_as)


def setup_inputs(seed: int = 0, part: int = 0) -> dict:
    keys = jax.random.split(jax.random.key(seed), 13)
    own_keys = jax.random.split(jax.random.fold_in(keys[12], part), 13)
    enc_tokens = draw_enc_tokens(jax.random.fold_in(jax.random.fold_in(keys[12], part), 71), part)
    pairs = draw_pairs(jax.random.fold_in(jax.random.fold_in(keys[12], part), 71), part)
    live = draw_live(jax.random.fold_in(jax.random.fold_in(keys[12], part), 71), part)
    proj_w = noise(keys[3], (E, D), E ** -0.5, 0.1875)
    self_qkv = draw_self_qkv(jax.random.fold_in(keys[12], 71), part)
    self_out = noise(keys[5], (D, D), D ** -0.5, 0.21875, ((0, 2),))
    cross_q = draw_cross_q(jax.random.fold_in(keys[12], 71), part)
    cross_kv = draw_cross_kv(jax.random.fold_in(keys[12], 71), part)
    cross_out = noise(keys[8], (D, D), D ** -0.5, 0.21875, ((0, 2),))
    mlp_w1 = noise(keys[9], (D, FF), D ** -0.5, 0.21875, ((1, 2),))
    mlp_w2 = noise(keys[10], (FF, D), FF ** -0.5, 0.109375, ((0, 2),))
    head_w = noise(keys[11], (D, OUTC), D ** -0.5, 0.21875, ((0, 8), (1, 2)))
    return {"enc_tokens": enc_tokens, "pairs": pairs, "live": live, "proj_w": proj_w, "self_qkv": self_qkv, "self_out": self_out, "cross_q": cross_q, "cross_kv": cross_kv, "cross_out": cross_out, "mlp_w1": mlp_w1, "mlp_w2": mlp_w2, "head_w": head_w}


eps_norm = 1e-06

def normed(tensor):
    tensor = tensor.astype(jnp.float32)
    center = tensor - lax.optimization_barrier(jnp.mean(tensor, axis=-1, keepdims=True))
    moment = lax.optimization_barrier(jnp.mean(center * center, axis=-1, keepdims=True))
    return center * lax.rsqrt(moment + eps_norm)

def attention(queries, key_rows, values):
    item_count, tok_count, feat_width = queries.shape
    head_count = feat_width // HD
    queries = queries.astype(jnp.float32).reshape(item_count, tok_count, head_count, HD)
    key_rows = key_rows.astype(jnp.float32).reshape(item_count, tok_count, head_count, HD)
    values = values.astype(jnp.float32).reshape(item_count, tok_count, head_count, HD)
    scores = jnp.einsum('bqhd,bkhd->bhqk', queries, key_rows) * HD ** (-0.5)
    biggest = lax.optimization_barrier(jnp.max(scores, axis=-1, keepdims=True))
    raised = jnp.exp(scores - biggest)
    softmax_w = (raised / lax.optimization_barrier(jnp.sum(raised, axis=-1, keepdims=True))).astype(jnp.bfloat16)
    context = jnp.einsum('bhqk,bkhd->bqhd', softmax_w.astype(jnp.float32), values)
    return context.astype(jnp.bfloat16).reshape(item_count, tok_count, feat_width)

def decode_block(tokens, partner, self_qkv, self_out, cross_q, cross_kv, cross_out, mlp_w1, mlp_w2, head_w):
    item_count, tok_count, feat_width = tokens.shape
    flat_rows = item_count * tok_count
    self_in = normed(tokens).astype(jnp.bfloat16).reshape(flat_rows, feat_width)
    triple = jnp.dot(self_in, self_qkv.reshape(feat_width, 3 * feat_width), preferred_element_type=jnp.float32)
    triple = triple.astype(jnp.bfloat16).reshape(item_count, tok_count, 3, feat_width)
    context = attention(triple[:, :, 0], triple[:, :, 1], triple[:, :, 2])
    after_self = tokens.reshape(flat_rows, feat_width).astype(jnp.float32) + jnp.dot(context.reshape(flat_rows, feat_width), self_out, preferred_element_type=jnp.float32)
    after_self = after_self.astype(jnp.bfloat16)
    asking = jnp.dot(normed(after_self).astype(jnp.bfloat16), cross_q, preferred_element_type=jnp.float32)
    asking = asking.astype(jnp.bfloat16).reshape(item_count, tok_count, feat_width)
    partner_in = normed(partner).astype(jnp.bfloat16).reshape(flat_rows, feat_width)
    seen_kv = jnp.dot(partner_in, cross_kv.reshape(feat_width, 2 * feat_width), preferred_element_type=jnp.float32)
    seen_kv = seen_kv.astype(jnp.bfloat16).reshape(item_count, tok_count, 2, feat_width)
    context = attention(asking, seen_kv[:, :, 0], seen_kv[:, :, 1])
    after_cross = after_self.astype(jnp.float32) + jnp.dot(context.reshape(flat_rows, feat_width), cross_out, preferred_element_type=jnp.float32)
    after_cross = after_cross.astype(jnp.bfloat16)
    mlp_in = normed(after_cross).astype(jnp.bfloat16)
    mlp_hidden = jax.nn.gelu(jnp.dot(mlp_in, mlp_w1, preferred_element_type=jnp.float32), approximate=False)
    mlp_hidden = mlp_hidden.astype(jnp.bfloat16)
    after_mlp = after_cross.astype(jnp.float32) + jnp.dot(mlp_hidden, mlp_w2, preferred_element_type=jnp.float32)
    after_mlp = after_mlp.astype(jnp.bfloat16)
    head_rows = jnp.dot(normed(after_mlp).astype(jnp.bfloat16), head_w, preferred_element_type=jnp.float32)
    return head_rows.reshape(item_count, tok_count, head_w.shape[1])

def reference(enc_tokens, pairs, live, proj_w, self_qkv, self_out, cross_q, cross_kv, cross_out, mlp_w1, mlp_w2, head_w):
    projected = jnp.dot(enc_tokens.reshape(IMAGES * TOK, E), proj_w, preferred_element_type=jnp.float32)
    projected = projected.astype(jnp.bfloat16).reshape(IMAGES, TOK, D)
    pair_table = pairs.reshape(N_IMG, 2 * CAP)

    def owner_step(carry, inputs):
        totals, counts = carry
        slot_images, slot_live = inputs
        tokens = jnp.take(projected, slot_images, axis=0)
        partner = tokens.reshape(CAP, 2, TOK, D)[:, ::-1].reshape(2 * CAP, TOK, D)
        head_rows = decode_block(tokens, partner, self_qkv, self_out, cross_q, cross_kv, cross_out, mlp_w1, mlp_w2, head_w)
        keep = (jnp.arange(2 * CAP) // 2 < slot_live).astype(jnp.float32)
        totals = totals.at[slot_images].add(head_rows * keep[:, None, None])
        counts = counts.at[slot_images].add(keep)
        return ((totals, counts), None)
    start_carry = (jnp.zeros((IMAGES, TOK, OUTC), jnp.float32), jnp.zeros((IMAGES,), jnp.float32))
    (totals, counts), _ = lax.scan(owner_step, start_carry, (pair_table, live))
    return jnp.transpose(totals, (0, 2, 1)) / jnp.maximum(counts, 1.0)[:, None, None]
```

```python
import jax
import jax.numpy as jnp
from jax import lax
from jax.sharding import PartitionSpec as P

HD = 64


eps_norm = 1e-06


def normed(tensor):
    tensor = tensor.astype(jnp.float32)
    center = tensor - jnp.mean(tensor, axis=-1, keepdims=True)
    moment = jnp.mean(center * center, axis=-1, keepdims=True)
    return center * lax.rsqrt(moment + eps_norm)


def attention(queries, key_rows, values):
    item_count, tok_count, feat_width = queries.shape
    head_count = feat_width // HD
    queries = queries.reshape(item_count, tok_count, head_count, HD)
    key_rows = key_rows.reshape(item_count, tok_count, head_count, HD)
    values = values.reshape(item_count, tok_count, head_count, HD)
    scores = jnp.einsum(
        "bqhd,bkhd->bhqk", queries, key_rows, preferred_element_type=jnp.float32
    ) * HD ** (-0.5)
    biggest = jnp.max(scores, axis=-1, keepdims=True)
    raised = jnp.exp(scores - biggest)
    softmax_w = (raised / jnp.sum(raised, axis=-1, keepdims=True)).astype(jnp.bfloat16)
    context = jnp.einsum("bhqk,bkhd->bqhd", softmax_w, values, preferred_element_type=jnp.float32)
    return context.astype(jnp.bfloat16).reshape(item_count, tok_count, feat_width)


def add_branch(residual, context, w_out):
    item_count, tok_count, feat_width = residual.shape
    flat_rows = item_count * tok_count
    flat_ctx = context.reshape(flat_rows, context.shape[-1])
    summed = lax.psum_scatter(
        jnp.dot(flat_ctx, w_out, preferred_element_type=jnp.float32),
        "head",
        scatter_dimension=0,
        tiled=True,
    )
    share_rows = summed.shape[0]
    residual_rows = lax.dynamic_slice_in_dim(
        residual.reshape(flat_rows, feat_width), lax.axis_index("head") * share_rows, share_rows, 0
    )
    updated = (residual_rows.astype(jnp.float32) + summed).astype(jnp.bfloat16)
    gathered = lax.all_gather(updated, "head", axis=0, tiled=True)
    return gathered.reshape(item_count, tok_count, feat_width)


def decode_block(tokens, weights):
    self_qkv, self_out, cross_q, cross_kv, cross_out, mlp_w1, mlp_w2 = weights
    item_count, tok_count, feat_width = tokens.shape
    flat_rows = item_count * tok_count
    local_width = self_qkv.shape[2]
    partner = tokens.reshape(item_count // 2, 2, tok_count, feat_width)[:, ::-1].reshape(
        item_count, tok_count, feat_width
    )
    self_in = normed(tokens).astype(jnp.bfloat16).reshape(flat_rows, feat_width)
    triple = jnp.dot(
        self_in, self_qkv.reshape(feat_width, 3 * local_width), preferred_element_type=jnp.float32
    )
    triple = triple.astype(jnp.bfloat16).reshape(item_count, tok_count, 3, local_width)
    context = attention(triple[:, :, 0], triple[:, :, 1], triple[:, :, 2])
    after_self = add_branch(tokens, context, self_out)
    asking_in = normed(after_self).astype(jnp.bfloat16).reshape(flat_rows, feat_width)
    asking = jnp.dot(asking_in, cross_q, preferred_element_type=jnp.float32)
    asking = asking.astype(jnp.bfloat16).reshape(item_count, tok_count, local_width)
    partner_in = normed(partner).astype(jnp.bfloat16).reshape(flat_rows, feat_width)
    seen_kv = jnp.dot(
        partner_in,
        cross_kv.reshape(feat_width, 2 * local_width),
        preferred_element_type=jnp.float32,
    )
    seen_kv = seen_kv.astype(jnp.bfloat16).reshape(item_count, tok_count, 2, local_width)
    context = attention(asking, seen_kv[:, :, 0], seen_kv[:, :, 1])
    after_cross = add_branch(after_self, context, cross_out)
    mlp_in = normed(after_cross).astype(jnp.bfloat16).reshape(flat_rows, feat_width)
    mlp_hidden = jax.nn.gelu(
        jnp.dot(mlp_in, mlp_w1, preferred_element_type=jnp.float32), approximate=False
    )
    mlp_hidden = mlp_hidden.astype(jnp.bfloat16).reshape(item_count, tok_count, mlp_w1.shape[1])
    after_mlp = add_branch(after_cross, mlp_hidden, mlp_w2)
    final_in = normed(after_mlp).astype(jnp.bfloat16).reshape(flat_rows, feat_width)
    return final_in.reshape(item_count, tok_count, feat_width)


def on_device(
    enc_tokens,
    pairs,
    live,
    proj_w,
    self_qkv,
    self_out,
    cross_q,
    cross_kv,
    cross_out,
    mlp_w1,
    mlp_w2,
    head_w,
):
    img_count = lax.axis_size("img")
    my_index = lax.axis_index("img")
    img_dev, tok_count, enc_width = enc_tokens.shape
    slot_cap = pairs.shape[0] // img_count
    entry_total = 2 * slot_cap
    slot_most = (entry_total + img_count - 1) // img_count
    pair_table = pairs.reshape(img_count, entry_total)
    entry_ids = jnp.arange(entry_total)
    active_full = entry_ids[None, :] // 2 < live[:, None]
    my_images = my_index * img_dev + jnp.arange(img_dev)
    counts = jnp.sum(
        ((pair_table[:, :, None] == my_images[None, None, :]) & active_full[:, :, None]).astype(
            jnp.float32
        ),
        axis=(0, 1),
    )
    weights = (self_qkv, self_out, cross_q, cross_kv, cross_out, mlp_w1, mlp_w2)
    source = pair_table // img_dev
    within = pair_table % img_dev
    mine_mask = (source == my_index) & active_full
    send_rank = jnp.cumsum(mine_mask.astype(jnp.int32), axis=1) - 1
    send_hit = (
        mine_mask[:, :, None, None]
        & (send_rank[:, :, None, None] == jnp.arange(slot_most)[None, None, :, None])
        & (within[:, :, None, None] == jnp.arange(img_dev)[None, None, None, :])
    )
    sender = jnp.sum(send_hit.astype(jnp.float32), axis=1).reshape(img_count * slot_most, img_dev)
    head_full = lax.all_gather(head_w, "img", axis=0, tiled=True)
    projected = jnp.dot(
        enc_tokens.reshape(img_dev * tok_count, enc_width),
        proj_w,
        preferred_element_type=jnp.float32,
    ).astype(jnp.bfloat16)
    payload = projected.reshape(img_dev, tok_count * proj_w.shape[1])
    outgoing = jnp.dot(sender.astype(jnp.bfloat16), payload, preferred_element_type=jnp.float32)
    outgoing = outgoing.astype(jnp.bfloat16).reshape(
        img_count, slot_most, tok_count, payload.shape[1] // tok_count
    )
    incoming = lax.all_to_all(outgoing, "img", split_axis=0, concat_axis=0, tiled=True)
    my_pairs = lax.dynamic_index_in_dim(pair_table, my_index, 0, keepdims=False)
    my_active = lax.dynamic_index_in_dim(active_full, my_index, 0, keepdims=False)
    my_source = my_pairs // img_dev
    before = (
        (my_source[None, :] == my_source[:, None])
        & my_active[None, :]
        & (entry_ids[None, :] < entry_ids[:, None])
    )
    recv_rank = jnp.sum(before.astype(jnp.int32), axis=1)
    pick_mask = (
        my_active[:, None, None]
        & (my_source[:, None, None] == jnp.arange(img_count)[None, :, None])
        & (recv_rank[:, None, None] == jnp.arange(slot_most)[None, None, :])
    )
    pick_mask = pick_mask.reshape(entry_total, img_count * slot_most).astype(jnp.float32)
    arrived_tokens = jnp.dot(
        pick_mask.astype(jnp.bfloat16),
        incoming.reshape(img_count * slot_most, -1),
        preferred_element_type=jnp.float32,
    )
    tokens = arrived_tokens.astype(jnp.bfloat16)
    tokens = tokens.reshape(entry_total, tok_count, proj_w.shape[1])
    final_in = decode_block(tokens, weights)
    flat_out = final_in.reshape(entry_total, -1)
    returned = jnp.dot(
        pick_mask.T.astype(jnp.bfloat16), flat_out, preferred_element_type=jnp.float32
    ).astype(jnp.bfloat16)
    returned = returned.reshape(img_count, slot_most, flat_out.shape[1])
    arrived = lax.all_to_all(returned, "img", split_axis=0, concat_axis=0, tiled=True).reshape(
        img_count * slot_most, -1
    )
    totals = jnp.dot(
        sender.T.astype(jnp.bfloat16), arrived, preferred_element_type=jnp.float32
    ).reshape(img_dev, tok_count, -1)
    coarse = lax.reduce_precision(totals, 8, 7)
    both = jnp.concatenate([coarse, totals - coarse], axis=1).astype(jnp.bfloat16)
    rows = jnp.einsum("ind,dc->icn", both, head_full, preferred_element_type=jnp.float32)
    rows = rows[:, :, :tok_count] + rows[:, :, tok_count:]
    return rows / jnp.maximum(counts, 1.0)[:, None, None]


def solution(mesh):
    placed = (
        P(("groups", "img"), None, None),
        P("groups", None),
        P("groups"),
        P(),
        P(None, None, "head"),
        P("head", None),
        P(None, "head"),
        P(None, None, "head"),
        P("head", None),
        P(None, "head"),
        P("head", None),
        P("img", "head"),
    )
    return jax.shard_map(
        on_device,
        mesh=mesh,
        in_specs=placed,
        out_specs=P(("groups", "img"), "head", None),
        check_vma=False,
    )
```

```python
import functools

import jax
import jax.numpy as jnp
from jax import lax
from jax.experimental import pallas as pl
from jax.experimental.pallas import tpu as pltpu
from jax.sharding import PartitionSpec as P

HD = 64
EPS_NORM = 1e-06
F32 = jnp.float32
BF16 = jnp.bfloat16
MESH = pl.DeviceIdType.MESH


def normed(tensor):
    tensor = tensor.astype(F32)
    center = tensor - jnp.mean(tensor, axis=-1, keepdims=True)
    moment = jnp.mean(center * center, axis=-1, keepdims=True)
    return center * lax.rsqrt(moment + EPS_NORM)


def mm(a, b):
    return jnp.dot(a, b, preferred_element_type=F32)


def gelu(x):
    return 0.5 * x * (1.0 + lax.erf(x * (0.5**0.5)))


def attend(queries, key_rows, values, tok):
    rows, width = queries.shape
    row = lax.broadcasted_iota(jnp.int32, (rows, rows), 0) // tok
    col = lax.broadcasted_iota(jnp.int32, (rows, rows), 1) // tok
    same = row == col
    pair = 2 * HD
    first = lax.broadcasted_iota(jnp.int32, (1, pair), 1) < HD
    sides = (first.astype(F32).astype(BF16), 1 - first.astype(F32).astype(BF16))
    parts = []
    for at in range(0, width, pair):
        q2, k2, v2 = (x[:, at : at + pair] for x in (queries, key_rows, values))
        found = []
        for side in sides:
            scores = lax.dot_general(
                q2 * side, k2, (((1,), (1,)), ((), ())), preferred_element_type=F32
            )
            scores = jnp.where(same, scores * HD ** (-0.5), -jnp.inf)
            raised = jnp.exp(scores - jnp.max(scores, axis=-1, keepdims=True))
            probs = raised / jnp.sum(raised, axis=-1, keepdims=True)
            found.append(mm(probs.astype(BF16), v2))
        parts.append(jnp.where(first, found[0], found[1]).astype(BF16))
    return jnp.concatenate(parts, axis=1)


def kernel(
    n,
    ids_ref,
    sel_ref,
    enc_ref,
    proj_hbm,
    qkv_hbm,
    sout_hbm,
    cq_hbm,
    ckv_hbm,
    co_hbm,
    w1_hbm,
    w2_hbm,
    out_ref,
    proj,
    qkv,
    sout,
    cq,
    ckv,
    co,
    w1,
    w2,
    all_in,
    all_as,
    part_mine,
    part_theirs,
    asked,
    partner,
    fin,
    back_out,
    back_in,
    sums,
    load_sem,
    wsend_sem,
    wrecv_sem,
    gsend_sem,
    grecv_sem,
    fsend_sem,
    frecv_sem,
    bsend_sem,
    brecv_sem,
    xsend_sem,
    xrecv_sem,
):
    me = lax.axis_index("img")
    core = lax.axis_index("head")
    other = 1 - core
    img_dev, tok = all_in.shape[2], all_in.shape[3]
    rows = img_dev * tok
    width = out_ref.shape[1]
    half = width // 2
    count = asked.shape[0]
    sibling = {"head": other}

    def peer(step):
        return lax.rem(me + step, n)

    def remote(src, dst, send, recv, where):
        return pltpu.make_async_remote_copy(
            src_ref=src, dst_ref=dst, send_sem=send, recv_sem=recv, device_id=where,
            device_id_type=MESH,
        )

    hbm = (proj_hbm, qkv_hbm, sout_hbm, cq_hbm, ckv_hbm, co_hbm, w1_hbm, w2_hbm)
    dst = (proj, qkv, sout, cq.at[0], ckv.at[0], co.at[0], w1.at[0], w2.at[0])
    loads = [pltpu.make_async_copy(s, d, load_sem.at[i]) for i, (s, d) in enumerate(zip(hbm, dst))]
    for load in loads:
        load.start()

    barrier = pltpu.get_barrier_semaphore()
    pl.semaphore_signal(barrier, inc=1, device_id=sibling, device_id_type=MESH)

    @pl.loop(1, n)
    def _(step):
        pl.semaphore_signal(barrier, inc=1, device_id={"img": peer(step)}, device_id_type=MESH)

    pl.semaphore_wait(barrier, n)

    pieces = [
        remote(s, d.at[1], wsend_sem.at[i], wrecv_sem.at[i], sibling)
        for i, (s, d) in enumerate(
            ((cq_hbm, cq), (ckv_hbm, ckv), (co_hbm, co), (w1_hbm, w1), (w2_hbm, w2))
        )
    ]

    def spread(kind, ref):
        @pl.loop(1, n)
        def _(step):
            to = peer(step)
            remote(
                ref.at[me, core], ref.at[me, core], gsend_sem.at[kind, to],
                grecv_sem.at[kind, me], {"img": to},
            ).start()

    def forward(kind, ref):
        @pl.loop(1, n)
        def _(step):
            of = peer(step)
            block = ref.at[of, core]
            remote(
                block, block, gsend_sem.at[kind, of], grecv_sem.at[kind, of], {"img": of}
            ).wait_recv()
            remote(
                block, block, fsend_sem.at[kind, of], frecv_sem.at[kind, of], sibling
            ).start()

    def settle(kind, ref):
        @pl.loop(1, n)
        def _(step):
            of = peer(step)
            block = ref.at[of, other]
            remote(
                block, block, fsend_sem.at[kind, of], frecv_sem.at[kind, of], sibling
            ).wait_recv()

    def drain(kind, ref):
        @pl.loop(1, n)
        def _(step):
            of = peer(step)
            block = ref.at[me, core]
            remote(
                block, block, gsend_sem.at[kind, of], grecv_sem.at[kind, of], {"img": of}
            ).wait_send()
            block = ref.at[of, core]
            remote(
                block, block, fsend_sem.at[kind, of], frecv_sem.at[kind, of], sibling
            ).wait_send()

    def put(ref, value):
        for side in range(2):
            ref[me, side] = value[:, side * half : (side + 1) * half].reshape(img_dev, tok, half)

    loads[0].wait()
    tokens = mm(enc_ref[...], proj[...]).astype(BF16)
    self_in = normed(tokens).astype(BF16)
    put(all_in, self_in)
    spread(0, all_in)
    loads[1].wait()
    triple = mm(self_in, qkv[...]).astype(BF16)
    local = triple.shape[1] // 3
    context = attend(
        triple[:, :local], triple[:, local : 2 * local], triple[:, 2 * local :], tok
    )
    loads[2].wait()
    part_mine[...] = mm(context, sout[...])
    swap = remote(part_mine, part_theirs, xsend_sem.at[0], xrecv_sem.at[0], sibling)
    swap.start()
    for piece in pieces:
        piece.start()
    swap.wait()
    after_self = (tokens.astype(F32) + (part_mine[...] + part_theirs[...])).astype(BF16)
    put(all_as, after_self)
    spread(1, all_as)
    forward(0, all_in)
    forward(1, all_as)
    settle(0, all_in)
    settle(1, all_as)

    entries = count // tok

    @pl.loop(0, entries)
    def _(e):
        mine = ids_ref[core * entries + e]
        seen = ids_ref[core * entries + e + 1 - 2 * lax.rem(e, 2)]
        at = pl.ds(pl.multiple_of(e * tok, tok), tok)
        for side in range(2):
            lanes = slice(side * half, (side + 1) * half)
            asked[at, lanes] = all_as[mine // img_dev, side, lax.rem(mine, img_dev)]
            partner[at, lanes] = all_in[seen // img_dev, side, lax.rem(seen, img_dev)]

    for load in loads[3:]:
        load.wait()
    for piece in pieces:
        piece.wait()

    chunk = min(256, count)
    group = min(128, chunk)
    tile = 512

    @pl.loop(0, count // chunk)
    def _(step):
        at = pl.ds(pl.multiple_of(step * chunk, chunk), chunk)
        held = asked[at, :]
        query_in = normed(held).astype(BF16)
        seen_in = partner[at, :]

        def cross(side, total):
            asking = mm(query_in, cq[side]).astype(BF16)
            seen_kv = mm(seen_in, ckv[side]).astype(BF16)
            ctx = [
                attend(
                    asking[g : g + group], seen_kv[g : g + group, :local],
                    seen_kv[g : g + group, local:], tok,
                )
                for g in range(0, chunk, group)
            ]
            return total + mm(jnp.concatenate(ctx, axis=0), co[side])

        total = lax.fori_loop(0, 2, cross, held.astype(F32))
        after_cross = total.astype(BF16)
        mlp_in = normed(after_cross).astype(BF16)
        total = after_cross.astype(F32)
        for tile_at in range(0, w1.shape[2], tile):
            def hidden(side, total, tile_at=tile_at):
                up = gelu(mm(mlp_in, w1[side, :, tile_at : tile_at + tile])).astype(BF16)
                return total + mm(up, w2[side, tile_at : tile_at + tile, :])

            total = lax.fori_loop(0, 2, hidden, total)
        final_in = normed(total.astype(BF16)).astype(BF16)
        for side in range(2):
            fin[core, side, at, :] = final_in[:, side * half : (side + 1) * half]

    trade = remote(
        fin.at[core, other], fin.at[core, other], xsend_sem.at[1], xrecv_sem.at[1], sibling
    )
    trade.start()
    trade.wait_recv()

    row = lax.broadcasted_iota(jnp.int32, (rows, count), 0)
    col = lax.broadcasted_iota(jnp.int32, (rows, count), 1)
    aligned = lax.rem(row, tok) == lax.rem(col, tok)

    def gathered(owner):
        image = owner * img_dev + row // tok
        total = None
        for part in range(2):
            chosen = aligned & (sel_ref[:, part * count : (part + 1) * count] == image)
            term = mm(jnp.where(chosen, 1.0, 0.0).astype(BF16), fin[part, core])
            total = term if total is None else total + term
        return total

    @pl.loop(1, n)
    def _(step):
        to = peer(step)
        back_out[to] = gathered(to).astype(BF16)
        remote(
            back_out.at[to], back_in.at[me], bsend_sem.at[to], brecv_sem.at[me], {"img": to}
        ).start()

    sums[core] = gathered(me)

    @pl.loop(1, n)
    def _(step):
        of = peer(step)
        remote(
            back_out.at[of], back_in.at[of], bsend_sem.at[of], brecv_sem.at[of], {"img": of}
        ).wait_recv()
        sums[core] += back_in[of].astype(F32)

    last = remote(sums.at[core], sums.at[core], xsend_sem.at[2], xrecv_sem.at[2], sibling)
    last.start()
    last.wait()
    out_ref[:, :half] = sums[0]
    out_ref[:, half:] = sums[1]

    trade.wait_send()
    drain(0, all_in)
    drain(1, all_as)

    @pl.loop(1, n)
    def _(step):
        of = peer(step)
        remote(
            back_out.at[of], back_in.at[of], bsend_sem.at[of], brecv_sem.at[of], {"img": of}
        ).wait_send()


def on_device(
    enc_tokens,
    pairs,
    live,
    proj_w,
    self_qkv,
    self_out,
    cross_q,
    cross_kv,
    cross_out,
    mlp_w1,
    mlp_w2,
    head_w,
):
    n = lax.axis_size("img")
    me = lax.axis_index("img")
    img_dev, tok, enc_width = enc_tokens.shape
    rows = img_dev * tok
    width, local = cross_q.shape
    half = width // 2
    entry_total = 2 * pairs.shape[0] // n
    table = pairs.reshape(n, entry_total)
    active = jnp.arange(entry_total)[None, :] // 2 < live[:, None]
    my_images = me * img_dev + jnp.arange(img_dev)
    named = (table[:, :, None] == my_images[None, None, :]) & active[:, :, None]
    counts = jnp.sum(named.astype(F32), axis=(0, 1))
    ids = lax.dynamic_index_in_dim(table, me, 0, keepdims=False)
    on = lax.dynamic_index_in_dim(active, me, 0, keepdims=False)
    sel = jnp.repeat(jnp.where(on, ids, -1), tok)[None, :]
    head_full = lax.all_gather(head_w, "img", axis=0, tiled=True)

    count = entry_total * tok // 2
    hidden = mlp_w1.shape[1]
    vmem = pl.BlockSpec(memory_space=pltpu.VMEM)
    sem = pltpu.SemaphoreType.DMA
    anywhere = pl.BlockSpec(memory_space=pl.ANY)
    totals = pl.pallas_call(
        functools.partial(kernel, n),
        out_shape=jax.ShapeDtypeStruct((rows, width), F32),
        in_specs=[pl.BlockSpec(memory_space=pltpu.SMEM), vmem, vmem] + [anywhere] * 8,
        out_specs=vmem,
        scratch_shapes=[
            pltpu.VMEM(proj_w.shape, BF16),
            pltpu.VMEM((width, 3 * local), BF16),
            pltpu.VMEM(self_out.shape, BF16),
            pltpu.VMEM((2, width, local), BF16),
            pltpu.VMEM((2, width, 2 * local), BF16),
            pltpu.VMEM((2, local, width), BF16),
            pltpu.VMEM((2, width, hidden), BF16),
            pltpu.VMEM((2, hidden, width), BF16),
            pltpu.VMEM((n, 2, img_dev, tok, half), BF16),
            pltpu.VMEM((n, 2, img_dev, tok, half), BF16),
            pltpu.VMEM((rows, width), F32),
            pltpu.VMEM((rows, width), F32),
            pltpu.VMEM((count, width), BF16),
            pltpu.VMEM((count, width), BF16),
            pltpu.VMEM((2, 2, count, half), BF16),
            pltpu.VMEM((n, rows, half), BF16),
            pltpu.VMEM((n, rows, half), BF16),
            pltpu.VMEM((2, rows, half), F32),
            sem((8,)),
            sem((5,)),
            sem((5,)),
            sem((2, n)),
            sem((2, n)),
            sem((2, n)),
            sem((2, n)),
            sem((n,)),
            sem((n,)),
            sem((3,)),
            sem((3,)),
        ],
        compiler_params=pltpu.CompilerParams(
            collective_id=0, has_side_effects=True, vmem_limit_bytes=56 * 1024 * 1024
        ),
        cost_estimate=pl.CostEstimate(
            flops=12_000_000_000, bytes_accessed=20_000_000, transcendentals=2_000_000
        ),
    )(
        ids,
        sel,
        enc_tokens.reshape(rows, enc_width),
        proj_w,
        self_qkv.reshape(width, 3 * local),
        self_out,
        cross_q,
        cross_kv.reshape(width, 2 * local),
        cross_out,
        mlp_w1,
        mlp_w2,
    )
    totals = totals.reshape(img_dev, tok, width)
    coarse = lax.reduce_precision(totals, 8, 7)
    both = jnp.concatenate([coarse, totals - coarse], axis=1).astype(BF16)
    out = jnp.einsum("ind,dc->inc", both, head_full, preferred_element_type=F32)
    out = (out[:, :tok] + out[:, tok:]) / jnp.maximum(counts, 1.0)[:, None, None]
    return jnp.transpose(out, (0, 2, 1))


def solution(mesh):
    placed = (
        P(("groups", "img"), None, None),
        P("groups", None),
        P("groups"),
        P(),
        P(None, None, "head"),
        P("head", None),
        P(None, "head"),
        P(None, None, "head"),
        P("head", None),
        P(None, "head"),
        P("head", None),
        P("img", "head"),
    )
    return jax.shard_map(
        on_device,
        mesh=mesh,
        in_specs=placed,
        out_specs=P(("groups", "img"), "head", None),
        check_vma=False,
    )
```

```python
import functools

import jax
import jax.numpy as jnp
from jax import lax
from jax.experimental import pallas as pl
from jax.experimental.pallas import tpu as pltpu
from jax.sharding import PartitionSpec as P

HD = 64
EPS_NORM = 1e-06
F32 = jnp.float32
BF16 = jnp.bfloat16
MESH = pl.DeviceIdType.MESH


def normed(tensor):
    tensor = tensor.astype(F32)
    center = tensor - jnp.mean(tensor, axis=-1, keepdims=True)
    moment = jnp.mean(center * center, axis=-1, keepdims=True)
    return center * lax.rsqrt(moment + EPS_NORM)


def mm(a, b):
    return jnp.dot(a, b, preferred_element_type=F32)


def gelu(x):
    return 0.5 * x * (1.0 + lax.erf(x * (0.5**0.5)))


def attend(queries, key_rows, values, tok):
    rows, width = queries.shape
    row = lax.broadcasted_iota(jnp.int32, (rows, rows), 0) // tok
    col = lax.broadcasted_iota(jnp.int32, (rows, rows), 1) // tok
    same = row == col
    pair = 2 * HD
    first = lax.broadcasted_iota(jnp.int32, (1, pair), 1) < HD
    sides = (first.astype(F32).astype(BF16), 1 - first.astype(F32).astype(BF16))
    parts = []
    for at in range(0, width, pair):
        q2, k2, v2 = (x[:, at : at + pair] for x in (queries, key_rows, values))
        found = []
        for side in sides:
            scores = lax.dot_general(
                q2 * side, k2, (((1,), (1,)), ((), ())), preferred_element_type=F32
            )
            scores = jnp.where(same, scores * HD ** (-0.5), -jnp.inf)
            raised = jnp.exp(scores - jnp.max(scores, axis=-1, keepdims=True))
            probs = raised / jnp.sum(raised, axis=-1, keepdims=True)
            found.append(mm(probs.astype(BF16), v2))
        parts.append(jnp.where(first, found[0], found[1]).astype(BF16))
    return jnp.concatenate(parts, axis=1)


def kernel(
    n,
    ids_ref,
    sel_ref,
    enc_ref,
    proj_hbm,
    qkv_hbm,
    sout_hbm,
    cq_hbm,
    ckv_hbm,
    co_hbm,
    w1_hbm,
    w2_hbm,
    head_hbm,
    out_ref,
    head_ref,
    proj,
    qkv,
    sout,
    cq,
    ckv,
    co,
    w1,
    w2,
    all_in,
    all_as,
    part_mine,
    part_theirs,
    asked,
    partner,
    fin,
    back_out,
    across,
    back_in,
    sums,
    load_sem,
    hload_sem,
    wsend_sem,
    wrecv_sem,
    gsend_sem,
    grecv_sem,
    ysend_sem,
    fsend_sem,
    frecv_sem,
    bsend_sem,
    arecv_sem,
    brecv_sem,
    xsend_sem,
    xrecv_sem,
):
    me = lax.axis_index("img")
    core = lax.axis_index("head")
    other = 1 - core
    img_dev, tok = all_in.shape[2], all_in.shape[3]
    rows = img_dev * tok
    width = out_ref.shape[1]
    half = width // 2
    count = asked.shape[0]
    sibling = {"head": other}

    lines = n // 2
    line, lane = me // 2, lax.rem(me, 2)
    mate = me + 1 - 2 * lane

    def peer(step):
        return lax.rem(line + step, lines) * 2 + lane

    def remote(src, dst, send, recv, where):
        return pltpu.make_async_remote_copy(
            src_ref=src, dst_ref=dst, send_sem=send, recv_sem=recv, device_id=where,
            device_id_type=MESH,
        )

    hbm = (proj_hbm, qkv_hbm, sout_hbm, cq_hbm, ckv_hbm, co_hbm, w1_hbm, w2_hbm)
    dst = (proj, qkv, sout, cq.at[0], ckv.at[0], co.at[0], w1.at[0], w2.at[0])
    loads = [pltpu.make_async_copy(s, d, load_sem.at[i]) for i, (s, d) in enumerate(zip(hbm, dst))]
    for load in loads:
        load.start()

    barrier = pltpu.get_barrier_semaphore()
    pl.semaphore_signal(barrier, inc=1, device_id=sibling, device_id_type=MESH)

    pl.semaphore_signal(barrier, inc=1, device_id={"img": mate}, device_id_type=MESH)

    @pl.loop(1, lines)
    def _(step):
        pl.semaphore_signal(barrier, inc=1, device_id={"img": peer(step)}, device_id_type=MESH)

    pl.semaphore_wait(barrier, lines + 1)

    pieces = [
        remote(s, d.at[1], wsend_sem.at[i], wrecv_sem.at[i], sibling)
        for i, (s, d) in enumerate(
            ((cq_hbm, cq), (ckv_hbm, ckv), (co_hbm, co), (w1_hbm, w1), (w2_hbm, w2))
        )
    ]

    def spread(kind, src, view):
        @pl.loop(1, lines)
        def _(step):
            to = peer(step)
            remote(
                src, view(me), gsend_sem.at[kind, to], grecv_sem.at[kind, me], {"img": to}
            ).start()

        remote(
            src, view(me), gsend_sem.at[kind, mate], grecv_sem.at[kind, me], {"img": mate}
        ).start()

    def arrival(kind, view, of):
        remote(
            view(of), view(of), gsend_sem.at[kind, of], grecv_sem.at[kind, of], {"img": mate}
        ).wait_recv()

    def crossing(kind, view, of):
        return remote(
            view(of), view(of), ysend_sem.at[kind, of], grecv_sem.at[kind, of], {"img": mate}
        )

    def handing(kind, view, of):
        return remote(
            view(of), view(of), fsend_sem.at[kind, of], frecv_sem.at[kind, of], sibling
        )

    def forward(kind, view, hand=True):
        @pl.loop(1, lines)
        def _(step):
            of = peer(step)
            arrival(kind, view, of)
            crossing(kind, view, of).start()
            if hand:
                handing(kind, view, of).start()

    def settle(kind, view, hand=True):
        @pl.loop(0, lines)
        def _(step):
            of = peer(step) + 1 - 2 * lane
            arrival(kind, view, of)
            if hand:
                handing(kind, view, of).start()

    def receive(kind, view):
        @pl.loop(1, n)
        def _(step):
            handing(kind, view, lax.rem(me + step, n)).wait_recv()

    def drain(kind, view, hand=True):
        @pl.loop(1, lines)
        def _(step):
            to = peer(step)
            remote(
                view(me), view(me), gsend_sem.at[kind, to], grecv_sem.at[kind, me], {"img": to}
            ).wait_send()
            crossing(kind, view, to).wait_send()

        remote(
            view(me), view(me), gsend_sem.at[kind, mate], grecv_sem.at[kind, me], {"img": mate}
        ).wait_send()
        if hand:
            @pl.loop(1, n)
            def _(step):
                handing(kind, view, lax.rem(me + step, n)).wait_send()

    def in_view(side):
        return lambda of: all_in.at[of, side]

    def as_view(side):
        return lambda of: all_as.at[of, side]

    def head_view(of):
        return head_ref.at[of]

    own_head = pltpu.make_async_copy(head_hbm, head_ref.at[me], hload_sem.at[0])
    own_head.start()

    def put(ref, value):
        for side in range(2):
            ref[me, side] = value[:, side * half : (side + 1) * half].reshape(img_dev, tok, half)

    loads[0].wait()
    tokens = mm(enc_ref[...], proj[...]).astype(BF16)
    self_in = normed(tokens).astype(BF16)
    put(all_in, self_in)
    spread(0, all_in.at[me, core], in_view(core))
    loads[1].wait()
    triple = mm(self_in, qkv[...]).astype(BF16)
    local = triple.shape[1] // 3
    context = attend(
        triple[:, :local], triple[:, local : 2 * local], triple[:, 2 * local :], tok
    )
    loads[2].wait()
    part_mine[...] = mm(context, sout[...])
    swap = remote(part_mine, part_theirs, xsend_sem.at[0], xrecv_sem.at[0], sibling)
    swap.start()
    for piece in pieces:
        piece.start()
    swap.wait()
    after_self = (tokens.astype(F32) + (part_mine[...] + part_theirs[...])).astype(BF16)
    put(all_as, after_self)
    spread(1, all_as.at[me, core], as_view(core))
    forward(0, in_view(core))
    forward(1, as_view(core))
    settle(0, in_view(core))
    settle(1, as_view(core))
    spread(2, head_hbm, head_view)
    receive(0, in_view(other))
    receive(1, as_view(other))

    entries = count // tok

    @pl.loop(0, entries)
    def _(e):
        mine = ids_ref[core * entries + e]
        seen = ids_ref[core * entries + e + 1 - 2 * lax.rem(e, 2)]
        at = pl.ds(pl.multiple_of(e * tok, tok), tok)
        for side in range(2):
            lanes = slice(side * half, (side + 1) * half)
            asked[at, lanes] = all_as[mine // img_dev, side, lax.rem(mine, img_dev)]
            partner[at, lanes] = all_in[seen // img_dev, side, lax.rem(seen, img_dev)]

    for load in loads[3:]:
        load.wait()
    for piece in pieces:
        piece.wait()

    chunk = min(256, count)
    group = min(128, chunk)
    tile = 512

    @pl.loop(0, count // chunk)
    def _(step):
        @pl.when(step == count // chunk - 1)
        def _():
            forward(2, head_view, hand=False)

        at = pl.ds(pl.multiple_of(step * chunk, chunk), chunk)
        held = asked[at, :]
        query_in = normed(held).astype(BF16)
        seen_in = partner[at, :]

        def cross(side, total):
            asking = mm(query_in, cq[side]).astype(BF16)
            seen_kv = mm(seen_in, ckv[side]).astype(BF16)
            ctx = [
                attend(
                    asking[g : g + group], seen_kv[g : g + group, :local],
                    seen_kv[g : g + group, local:], tok,
                )
                for g in range(0, chunk, group)
            ]
            return total + mm(jnp.concatenate(ctx, axis=0), co[side])

        total = lax.fori_loop(0, 2, cross, held.astype(F32))
        after_cross = total.astype(BF16)
        mlp_in = normed(after_cross).astype(BF16)
        total = after_cross.astype(F32)
        for tile_at in range(0, w1.shape[2], tile):
            def hidden(side, total, tile_at=tile_at):
                up = gelu(mm(mlp_in, w1[side, :, tile_at : tile_at + tile])).astype(BF16)
                return total + mm(up, w2[side, tile_at : tile_at + tile, :])

            total = lax.fori_loop(0, 2, hidden, total)
        final_in = normed(total.astype(BF16)).astype(BF16)
        for side in range(2):
            fin[core, side, at, :] = final_in[:, side * half : (side + 1) * half]

    trade = remote(
        fin.at[core, other], fin.at[core, other], xsend_sem.at[1], xrecv_sem.at[1], sibling
    )
    trade.start()
    trade.wait_recv()

    row = lax.broadcasted_iota(jnp.int32, (rows, count), 0)
    col = lax.broadcasted_iota(jnp.int32, (rows, count), 1)
    aligned = lax.rem(row, tok) == lax.rem(col, tok)

    def gathered(owner):
        image = owner * img_dev + row // tok
        total = None
        for part in range(2):
            chosen = aligned & (sel_ref[:, part * count : (part + 1) * count] == image)
            term = mm(jnp.where(chosen, 1.0, 0.0).astype(BF16), fin[part, core])
            total = term if total is None else total + term
        return total

    def over(block):
        return remote(
            back_out.at[block], across.at[block // 2], bsend_sem.at[block],
            arecv_sem.at[block // 2], {"img": mate},
        )

    def along(to):
        return remote(
            back_out.at[to], back_in.at[line], bsend_sem.at[to], brecv_sem.at[line], {"img": to}
        )

    @pl.loop(0, lines)
    def _(step):
        block = peer(step + 1) + 1 - 2 * lane
        back_out[block] = gathered(block).astype(BF16)
        over(block).start()

    def joined(block):
        total = gathered(block)
        over(block).wait_recv()
        return total + across[block // 2].astype(F32)

    @pl.loop(1, lines)
    def _(step):
        to = peer(step)
        back_out[to] = joined(to).astype(BF16)
        along(to).start()

    sums[core] = joined(me)

    @pl.loop(1, lines)
    def _(step):
        of = peer(step)
        remote(
            back_out.at[of], back_in.at[of // 2], bsend_sem.at[of], brecv_sem.at[of // 2],
            {"img": of},
        ).wait_recv()
        sums[core] += back_in[of // 2].astype(F32)

    last = remote(sums.at[core], sums.at[core], xsend_sem.at[2], xrecv_sem.at[2], sibling)
    last.start()
    last.wait()
    out_ref[:, :half] = sums[0]
    out_ref[:, half:] = sums[1]

    trade.wait_send()
    settle(2, head_view, hand=False)
    own_head.wait()
    drain(0, in_view(core))
    drain(1, as_view(core))
    drain(2, head_view, hand=False)

    @pl.loop(0, lines)
    def _(step):
        over(peer(step) + 1 - 2 * lane).wait_send()

    @pl.loop(1, lines)
    def _(step):
        along(peer(step)).wait_send()


def on_device(
    enc_tokens,
    pairs,
    live,
    proj_w,
    self_qkv,
    self_out,
    cross_q,
    cross_kv,
    cross_out,
    mlp_w1,
    mlp_w2,
    head_w,
):
    n = lax.axis_size("img")
    me = lax.axis_index("img")
    img_dev, tok, enc_width = enc_tokens.shape
    rows = img_dev * tok
    width, local = cross_q.shape
    half = width // 2
    entry_total = 2 * pairs.shape[0] // n
    table = pairs.reshape(n, entry_total)
    active = jnp.arange(entry_total)[None, :] // 2 < live[:, None]
    my_images = me * img_dev + jnp.arange(img_dev)
    named = (table[:, :, None] == my_images[None, None, :]) & active[:, :, None]
    counts = jnp.sum(named.astype(F32), axis=(0, 1))
    ids = lax.dynamic_index_in_dim(table, me, 0, keepdims=False)
    on = lax.dynamic_index_in_dim(active, me, 0, keepdims=False)
    sel = jnp.repeat(jnp.where(on, ids, -1), tok)[None, :]

    count = entry_total * tok // 2
    hidden = mlp_w1.shape[1]
    vmem = pl.BlockSpec(memory_space=pltpu.VMEM)
    sem = pltpu.SemaphoreType.DMA
    anywhere = pl.BlockSpec(memory_space=pl.ANY)
    totals, head_all = pl.pallas_call(
        functools.partial(kernel, n),
        out_shape=(
            jax.ShapeDtypeStruct((rows, width), F32),
            jax.ShapeDtypeStruct((n, *head_w.shape), BF16),
        ),
        in_specs=[pl.BlockSpec(memory_space=pltpu.SMEM), vmem, vmem] + [anywhere] * 9,
        out_specs=(vmem, anywhere),
        scratch_shapes=[
            pltpu.VMEM(proj_w.shape, BF16),
            pltpu.VMEM((width, 3 * local), BF16),
            pltpu.VMEM(self_out.shape, BF16),
            pltpu.VMEM((2, width, local), BF16),
            pltpu.VMEM((2, width, 2 * local), BF16),
            pltpu.VMEM((2, local, width), BF16),
            pltpu.VMEM((2, width, hidden), BF16),
            pltpu.VMEM((2, hidden, width), BF16),
            pltpu.VMEM((n, 2, img_dev, tok, half), BF16),
            pltpu.VMEM((n, 2, img_dev, tok, half), BF16),
            pltpu.VMEM((rows, width), F32),
            pltpu.VMEM((rows, width), F32),
            pltpu.VMEM((count, width), BF16),
            pltpu.VMEM((count, width), BF16),
            pltpu.VMEM((2, 2, count, half), BF16),
            pltpu.VMEM((n, rows, half), BF16),
            pltpu.VMEM((n // 2, rows, half), BF16),
            pltpu.VMEM((n // 2, rows, half), BF16),
            pltpu.VMEM((2, rows, half), F32),
            sem((8,)),
            sem((1,)),
            sem((5,)),
            sem((5,)),
            sem((3, n)),
            sem((3, n)),
            sem((3, n)),
            sem((2, n)),
            sem((2, n)),
            sem((n,)),
            sem((n // 2,)),
            sem((n // 2,)),
            sem((3,)),
            sem((3,)),
        ],
        compiler_params=pltpu.CompilerParams(
            collective_id=0, has_side_effects=True, vmem_limit_bytes=56 * 1024 * 1024
        ),
        cost_estimate=pl.CostEstimate(
            flops=12_000_000_000, bytes_accessed=20_000_000, transcendentals=2_000_000
        ),
    )(
        ids,
        sel,
        enc_tokens.reshape(rows, enc_width),
        proj_w,
        self_qkv.reshape(width, 3 * local),
        self_out,
        cross_q,
        cross_kv.reshape(width, 2 * local),
        cross_out,
        mlp_w1,
        mlp_w2,
        head_w,
    )
    head_full = head_all.reshape(width, head_w.shape[1])
    totals = totals.reshape(img_dev, tok, width)
    coarse = lax.reduce_precision(totals, 8, 7)
    both = jnp.concatenate([coarse, totals - coarse], axis=1).astype(BF16)
    out = jnp.einsum("ind,dc->inc", both, head_full, preferred_element_type=F32)
    out = (out[:, :tok] + out[:, tok:]) / jnp.maximum(counts, 1.0)[:, None, None]
    return jnp.transpose(out, (0, 2, 1))


def solution(mesh):
    placed = (
        P(("groups", "img"), None, None),
        P("groups", None),
        P("groups"),
        P(),
        P(None, None, "head"),
        P("head", None),
        P(None, "head"),
        P(None, None, "head"),
        P("head", None),
        P(None, "head"),
        P("head", None),
        P("img", "head"),
    )
    return jax.shard_map(
        on_device,
        mesh=mesh,
        in_specs=placed,
        out_specs=P(("groups", "img"), "head", None),
        check_vma=False,
    )
```

```python
import functools

import jax
import jax.numpy as jnp
from jax import lax
from jax.experimental import pallas as pl
from jax.experimental.pallas import tpu as pltpu
from jax.sharding import PartitionSpec as P

HD = 64
EPS_NORM = 1e-06
F32 = jnp.float32
BF16 = jnp.bfloat16
MESH = pl.DeviceIdType.MESH


def normed(tensor):
    tensor = tensor.astype(F32)
    center = tensor - jnp.mean(tensor, axis=-1, keepdims=True)
    moment = jnp.mean(center * center, axis=-1, keepdims=True)
    return center * lax.rsqrt(moment + EPS_NORM)


def mm(a, b):
    return jnp.dot(a, b, preferred_element_type=F32)


def gelu(x):
    return 0.5 * x * (1.0 + lax.erf(x * (0.5**0.5)))


def attend(queries, key_rows, values, tok):
    rows, width = queries.shape
    row = lax.broadcasted_iota(jnp.int32, (rows, rows), 0) // tok
    col = lax.broadcasted_iota(jnp.int32, (rows, rows), 1) // tok
    same = row == col
    pair = 2 * HD
    first = lax.broadcasted_iota(jnp.int32, (1, pair), 1) < HD
    scale = HD ** (-0.5)
    sides = [jnp.where(on, scale, 0.0).astype(BF16) for on in (first, ~first)]
    parts = []
    for at in range(0, width, pair):
        q2, k2, v2 = (x[:, at : at + pair] for x in (queries, key_rows, values))
        found = []
        for side in sides:
            scores = lax.dot_general(
                q2 * side, k2, (((1,), (1,)), ((), ())), preferred_element_type=F32
            )
            scores = jnp.where(same, scores, -jnp.inf)
            raised = jnp.exp(scores - jnp.max(scores, axis=-1, keepdims=True))
            probs = raised * (1.0 / jnp.sum(raised, axis=-1, keepdims=True))
            found.append(mm(probs.astype(BF16), v2))
        parts.append(jnp.where(first, found[0], found[1]).astype(BF16))
    return jnp.concatenate(parts, axis=1)


def kernel(
    n,
    ids_ref,
    sel_ref,
    enc_ref,
    proj_hbm,
    qkv_hbm,
    sout_hbm,
    cq_hbm,
    ckv_hbm,
    co_hbm,
    w1_hbm,
    w2_hbm,
    head_hbm,
    out_ref,
    head_ref,
    proj,
    qkv,
    sout,
    cq,
    ckv,
    co,
    w1,
    w2,
    all_in,
    all_as,
    part_mine,
    part_theirs,
    asked,
    partner,
    fin,
    back_out,
    across,
    back_in,
    sums,
    load_sem,
    hload_sem,
    wsend_sem,
    wrecv_sem,
    gsend_sem,
    grecv_sem,
    ysend_sem,
    fsend_sem,
    frecv_sem,
    bsend_sem,
    arecv_sem,
    brecv_sem,
    xsend_sem,
    xrecv_sem,
):
    me = lax.axis_index("img")
    core = lax.axis_index("head")
    other = 1 - core
    img_dev, tok = all_in.shape[2], all_in.shape[3]
    rows = img_dev * tok
    width = out_ref.shape[2]
    half = width // 2
    count = asked.shape[0]
    sibling = {"head": other}

    lines = n // 2
    line, lane = me // 2, lax.rem(me, 2)
    mate = me + 1 - 2 * lane

    def peer(step):
        return lax.rem(line + step, lines) * 2 + lane

    def remote(src, dst, send, recv, where):
        return pltpu.make_async_remote_copy(
            src_ref=src, dst_ref=dst, send_sem=send, recv_sem=recv, device_id=where,
            device_id_type=MESH,
        )

    hbm = (proj_hbm, qkv_hbm, sout_hbm, cq_hbm, ckv_hbm, co_hbm, w1_hbm, w2_hbm)
    dst = (proj, qkv, sout, cq.at[0], ckv.at[0], co.at[0], w1.at[0], w2.at[0])
    loads = [pltpu.make_async_copy(s, d, load_sem.at[i]) for i, (s, d) in enumerate(zip(hbm, dst))]
    for load in loads:
        load.start()

    barrier = pltpu.get_barrier_semaphore()
    pl.semaphore_signal(barrier, inc=1, device_id=sibling, device_id_type=MESH)

    pl.semaphore_signal(barrier, inc=1, device_id={"img": mate}, device_id_type=MESH)

    @pl.loop(1, lines)
    def _(step):
        pl.semaphore_signal(barrier, inc=1, device_id={"img": peer(step)}, device_id_type=MESH)

    pl.semaphore_wait(barrier, lines + 1)

    pieces = [
        remote(s, d.at[1], wsend_sem.at[i], wrecv_sem.at[i], sibling)
        for i, (s, d) in enumerate(
            ((cq_hbm, cq), (ckv_hbm, ckv), (co_hbm, co), (w1_hbm, w1), (w2_hbm, w2))
        )
    ]

    def spread(kind, src, view):
        @pl.loop(1, lines)
        def _(step):
            to = peer(step)
            remote(
                src, view(me), gsend_sem.at[kind, to], grecv_sem.at[kind, me], {"img": to}
            ).start()

        remote(
            src, view(me), gsend_sem.at[kind, mate], grecv_sem.at[kind, me], {"img": mate}
        ).start()

    def arrival(kind, view, of):
        remote(
            view(of), view(of), gsend_sem.at[kind, of], grecv_sem.at[kind, of], {"img": mate}
        ).wait_recv()

    def crossing(kind, view, of):
        return remote(
            view(of), view(of), ysend_sem.at[kind, of], grecv_sem.at[kind, of], {"img": mate}
        )

    def handing(kind, view, of):
        return remote(
            view(of), view(of), fsend_sem.at[kind, of], frecv_sem.at[kind, of], sibling
        )

    def forward(kind, view, hand=True):
        @pl.loop(1, lines)
        def _(step):
            of = peer(step)
            arrival(kind, view, of)
            crossing(kind, view, of).start()
            if hand:
                handing(kind, view, of).start()

    def settle(kind, view, hand=True):
        @pl.loop(0, lines)
        def _(step):
            of = peer(step) + 1 - 2 * lane
            arrival(kind, view, of)
            if hand:
                handing(kind, view, of).start()

    def receive(kind, view):
        @pl.loop(1, n)
        def _(step):
            handing(kind, view, lax.rem(me + step, n)).wait_recv()

    def drain(kind, view, hand=True):
        @pl.loop(1, lines)
        def _(step):
            to = peer(step)
            remote(
                view(me), view(me), gsend_sem.at[kind, to], grecv_sem.at[kind, me], {"img": to}
            ).wait_send()
            crossing(kind, view, to).wait_send()

        remote(
            view(me), view(me), gsend_sem.at[kind, mate], grecv_sem.at[kind, me], {"img": mate}
        ).wait_send()
        if hand:
            @pl.loop(1, n)
            def _(step):
                handing(kind, view, lax.rem(me + step, n)).wait_send()

    def in_view(side):
        return lambda of: all_in.at[of, side]

    def as_view(side):
        return lambda of: all_as.at[of, side]

    def head_view(of):
        return head_ref.at[of]

    own_head = pltpu.make_async_copy(head_hbm, head_ref.at[me], hload_sem.at[0])
    own_head.start()

    def put(ref, value):
        for side in range(2):
            ref[me, side] = value[:, side * half : (side + 1) * half].reshape(img_dev, tok, half)

    loads[0].wait()
    tokens = mm(enc_ref[...], proj[...]).astype(BF16)
    self_in = normed(tokens).astype(BF16)
    put(all_in, self_in)
    spread(0, all_in.at[me, core], in_view(core))
    loads[1].wait()
    triple = mm(self_in, qkv[...]).astype(BF16)
    local = triple.shape[1] // 3
    context = attend(
        triple[:, :local], triple[:, local : 2 * local], triple[:, 2 * local :], tok
    )
    loads[2].wait()
    part_mine[...] = mm(context, sout[...])
    swap = remote(part_mine, part_theirs, xsend_sem.at[0], xrecv_sem.at[0], sibling)
    swap.start()
    for piece in pieces:
        piece.start()
    swap.wait()
    after_self = (tokens.astype(F32) + (part_mine[...] + part_theirs[...])).astype(BF16)
    put(all_as, after_self)
    spread(1, all_as.at[me, core], as_view(core))
    forward(0, in_view(core))
    forward(1, as_view(core))
    settle(0, in_view(core))
    settle(1, as_view(core))
    spread(2, head_hbm, head_view)
    receive(0, in_view(other))
    receive(1, as_view(other))

    entries = count // tok

    @pl.loop(0, entries)
    def _(e):
        mine = ids_ref[core * entries + e]
        seen = ids_ref[core * entries + e + 1 - 2 * lax.rem(e, 2)]
        at = pl.ds(pl.multiple_of(e * tok, tok), tok)
        for side in range(2):
            lanes = slice(side * half, (side + 1) * half)
            asked[at, lanes] = all_as[mine // img_dev, side, lax.rem(mine, img_dev)]
            partner[at, lanes] = all_in[seen // img_dev, side, lax.rem(seen, img_dev)]

    for load in loads[3:]:
        load.wait()
    for piece in pieces:
        piece.wait()

    chunk = min(256, count)
    group = min(128, chunk)
    tile = 512

    @pl.loop(0, count // chunk)
    def _(step):
        @pl.when(step == count // chunk - 1)
        def _():
            forward(2, head_view, hand=False)

        at = pl.ds(pl.multiple_of(step * chunk, chunk), chunk)
        held = asked[at, :]
        query_in = normed(held).astype(BF16)
        seen_in = partner[at, :]

        def cross(side, total):
            asking = mm(query_in, cq[side]).astype(BF16)
            seen_kv = mm(seen_in, ckv[side]).astype(BF16)
            ctx = [
                attend(
                    asking[g : g + group], seen_kv[g : g + group, :local],
                    seen_kv[g : g + group, local:], tok,
                )
                for g in range(0, chunk, group)
            ]
            return total + mm(jnp.concatenate(ctx, axis=0), co[side])

        total = lax.fori_loop(0, 2, cross, held.astype(F32))
        after_cross = total.astype(BF16)
        mlp_in = normed(after_cross).astype(BF16)
        total = after_cross.astype(F32)
        for tile_at in range(0, w1.shape[2], tile):
            def hidden(side, total, tile_at=tile_at):
                up = gelu(mm(mlp_in, w1[side, :, tile_at : tile_at + tile])).astype(BF16)
                return total + mm(up, w2[side, tile_at : tile_at + tile, :])

            total = lax.fori_loop(0, 2, hidden, total)
        final_in = normed(total.astype(BF16)).astype(BF16)
        for side in range(2):
            fin[core, side, at, :] = final_in[:, side * half : (side + 1) * half]

    trade = remote(
        fin.at[core, other], fin.at[core, other], xsend_sem.at[1], xrecv_sem.at[1], sibling
    )
    trade.start()
    trade.wait_recv()

    row = lax.broadcasted_iota(jnp.int32, (rows, count), 0)
    col = lax.broadcasted_iota(jnp.int32, (rows, count), 1)
    aligned = lax.rem(row, tok) == lax.rem(col, tok)

    def gathered(owner):
        image = owner * img_dev + row // tok
        total = None
        for part in range(2):
            chosen = aligned & (sel_ref[:, part * count : (part + 1) * count] == image)
            term = mm(jnp.where(chosen, 1.0, 0.0).astype(BF16), fin[part, core])
            total = term if total is None else total + term
        return total

    def over(block):
        return remote(
            back_out.at[block], across.at[block // 2], bsend_sem.at[block],
            arecv_sem.at[block // 2], {"img": mate},
        )

    def along(to):
        return remote(
            back_out.at[to], back_in.at[line], bsend_sem.at[to], brecv_sem.at[line], {"img": to}
        )

    @pl.loop(0, lines)
    def _(step):
        block = peer(step + 1) + 1 - 2 * lane
        back_out[block] = gathered(block).astype(BF16)
        over(block).start()

    def joined(block):
        total = gathered(block)
        over(block).wait_recv()
        return total + across[block // 2].astype(F32)

    @pl.loop(1, lines)
    def _(step):
        to = peer(step)
        back_out[to] = joined(to).astype(BF16)
        along(to).start()

    sums[core] = joined(me)

    @pl.loop(1, lines)
    def _(step):
        of = peer(step)
        remote(
            back_out.at[of], back_in.at[of // 2], bsend_sem.at[of], brecv_sem.at[of // 2],
            {"img": of},
        ).wait_recv()
        sums[core] += back_in[of // 2].astype(F32)

    last = remote(sums.at[core], sums.at[core], xsend_sem.at[2], xrecv_sem.at[2], sibling)
    last.start()
    last.wait()
    for side in range(2):
        lanes = slice(side * half, (side + 1) * half)
        whole = sums[side]
        coarse = whole.astype(BF16)
        rest = (whole - coarse.astype(F32)).astype(BF16)
        out_ref[:, :tok, lanes] = coarse.reshape(img_dev, tok, half)
        out_ref[:, tok:, lanes] = rest.reshape(img_dev, tok, half)

    trade.wait_send()
    settle(2, head_view, hand=False)
    own_head.wait()
    drain(0, in_view(core))
    drain(1, as_view(core))
    drain(2, head_view, hand=False)

    @pl.loop(0, lines)
    def _(step):
        over(peer(step) + 1 - 2 * lane).wait_send()

    @pl.loop(1, lines)
    def _(step):
        along(peer(step)).wait_send()


def on_device(
    enc_tokens,
    pairs,
    live,
    proj_w,
    self_qkv,
    self_out,
    cross_q,
    cross_kv,
    cross_out,
    mlp_w1,
    mlp_w2,
    head_w,
):
    n = lax.axis_size("img")
    me = lax.axis_index("img")
    img_dev, tok, enc_width = enc_tokens.shape
    rows = img_dev * tok
    width, local = cross_q.shape
    half = width // 2
    entry_total = 2 * pairs.shape[0] // n
    table = pairs.reshape(n, entry_total)
    active = jnp.arange(entry_total)[None, :] // 2 < live[:, None]
    my_images = me * img_dev + jnp.arange(img_dev)
    named = (table[:, :, None] == my_images[None, None, :]) & active[:, :, None]
    counts = jnp.sum(named.astype(F32), axis=(0, 1))
    ids = lax.dynamic_index_in_dim(table, me, 0, keepdims=False)
    on = lax.dynamic_index_in_dim(active, me, 0, keepdims=False)
    sel = jnp.repeat(jnp.where(on, ids, -1), tok)[None, :]

    count = entry_total * tok // 2
    hidden = mlp_w1.shape[1]
    vmem = pl.BlockSpec(memory_space=pltpu.VMEM)
    sem = pltpu.SemaphoreType.DMA
    anywhere = pl.BlockSpec(memory_space=pl.ANY)
    both, head_all = pl.pallas_call(
        functools.partial(kernel, n),
        out_shape=(
            jax.ShapeDtypeStruct((img_dev, 2 * tok, width), BF16),
            jax.ShapeDtypeStruct((n, *head_w.shape), BF16),
        ),
        in_specs=[pl.BlockSpec(memory_space=pltpu.SMEM), vmem, vmem] + [anywhere] * 9,
        out_specs=(vmem, anywhere),
        scratch_shapes=[
            pltpu.VMEM(proj_w.shape, BF16),
            pltpu.VMEM((width, 3 * local), BF16),
            pltpu.VMEM(self_out.shape, BF16),
            pltpu.VMEM((2, width, local), BF16),
            pltpu.VMEM((2, width, 2 * local), BF16),
            pltpu.VMEM((2, local, width), BF16),
            pltpu.VMEM((2, width, hidden), BF16),
            pltpu.VMEM((2, hidden, width), BF16),
            pltpu.VMEM((n, 2, img_dev, tok, half), BF16),
            pltpu.VMEM((n, 2, img_dev, tok, half), BF16),
            pltpu.VMEM((rows, width), F32),
            pltpu.VMEM((rows, width), F32),
            pltpu.VMEM((count, width), BF16),
            pltpu.VMEM((count, width), BF16),
            pltpu.VMEM((2, 2, count, half), BF16),
            pltpu.VMEM((n, rows, half), BF16),
            pltpu.VMEM((n // 2, rows, half), BF16),
            pltpu.VMEM((n // 2, rows, half), BF16),
            pltpu.VMEM((2, rows, half), F32),
            sem((8,)),
            sem((1,)),
            sem((5,)),
            sem((5,)),
            sem((3, n)),
            sem((3, n)),
            sem((3, n)),
            sem((2, n)),
            sem((2, n)),
            sem((n,)),
            sem((n // 2,)),
            sem((n // 2,)),
            sem((3,)),
            sem((3,)),
        ],
        compiler_params=pltpu.CompilerParams(
            collective_id=0, has_side_effects=True, vmem_limit_bytes=56 * 1024 * 1024
        ),
        cost_estimate=pl.CostEstimate(
            flops=12_000_000_000, bytes_accessed=20_000_000, transcendentals=2_000_000
        ),
    )(
        ids,
        sel,
        enc_tokens.reshape(rows, enc_width),
        proj_w,
        self_qkv.reshape(width, 3 * local),
        self_out,
        cross_q,
        cross_kv.reshape(width, 2 * local),
        cross_out,
        mlp_w1,
        mlp_w2,
        head_w,
    )
    head_full = head_all.reshape(width, head_w.shape[1])
    out = jnp.einsum("ind,dc->inc", both, head_full, preferred_element_type=F32)
    out = (out[:, :tok] + out[:, tok:]) / jnp.maximum(counts, 1.0)[:, None, None]
    return jnp.transpose(out, (0, 2, 1))


def solution(mesh):
    placed = (
        P(("groups", "img"), None, None),
        P("groups", None),
        P("groups"),
        P(),
        P(None, None, "head"),
        P("head", None),
        P(None, "head"),
        P(None, None, "head"),
        P("head", None),
        P(None, "head"),
        P("head", None),
        P("img", "head"),
    )
    return jax.shard_map(
        on_device,
        mesh=mesh,
        in_specs=placed,
        out_specs=P(("groups", "img"), "head", None),
        check_vma=False,
    )
```
